32 devices in a mesh: groups: 2 (over x), dp: 16 (over z, y, core).
Axes of the slice: x: 2, y: 2, z: 4, core: 2. Of those that a mesh axis runs over, the one named last changes fastest.
Arguments:
- queries: bfloat16 [32, 2, 4096], P('dp'), may hold values from -6 to 6
- inv_hessian: bfloat16 [2, 4096, 4096], P(None, 'dp'), as said below
- train_grads: bfloat16 [16384, 2, 4096], P(('groups', 'dp')), parts along dimension 0, may hold values from -0.0625 to 0.0625
Outputs:
- scores: float32 [32, 16384], P(None, ('groups', 'dp')), parts along dimension 1
The draws below stay inside these ranges and needn't reach their ends.
There are 2 independent parts, one for each index of `groups`. The reference program is written for one: setup_inputs(seed, part) draws one part's arguments, and reference() takes and returns one part's arrays. A program takes and returns all parts, laid end to end along the dimension named above; an argument that names none is the same for every part. Nothing has to cross between parts.
Inputs may be any that keep to these rules, and one draw needn't show every extreme that they name: Each inv_hessian[l] is symmetric.
All inputs are finite; a program needn't handle non-finite values.
Results may differ from the reference program's by a relative error of at most 0.0029.
Values may be sent and summed in bfloat16 or wider, within the bound.
A program may use at most 128 MiB of HBM per device.

```python
import math
import jax
import jax.numpy as jnp
from jax import lax

D = 4096
LAYERS = 2
T_DEV = 512
NQ = 32
TRAIN = 8192
N_DP = 16


def draw_inv_hessian(key, part):
    key = jax.random.fold_in(key, 7)
    key_off, key_diag = jax.random.split(key, 2)
    base = jax.random.normal(key_off, (LAYERS, D, D), jnp.float32)
    off_diag = (base + jnp.swapaxes(base, 1, 2)) * (0.5 / math.sqrt(2.0 * D))
    diag_vals = jnp.exp(jax.random.uniform(key_diag, (LAYERS, D), jnp.float32, math.log(0.5), math.log(2.0)))
    index_row = lax.broadcasted_iota(jnp.int32, (D, D), 0)
    index_col = lax.broadcasted_iota(jnp.int32, (D, D), 1)
    eye_mask = (index_row == index_col).astype(jnp.float32)
    matrix = off_diag * (1.0 - eye_mask) + eye_mask * diag_vals[:, :, None]
    return matrix.astype(jnp.bfloat16)


def steps_of(rng, shape, cuts, least, largest):
    def one(dim, shards_of):
        heights = jax.random.uniform(jax.random.fold_in(jax.random.fold_in(rng, 6), dim), (shards_of,), jnp.float32, least / len(cuts), largest / len(cuts))
        return jnp.repeat(jnp.exp(heights), shape[dim] // shards_of).reshape((-1,) + (1,) * (len(shape) - dim - 1))

    level = one(*cuts[0])
    for cut in cuts[1:]:
        level = level * one(*cut)
    return level


def normal_values(key, dims, width, limit, pieces=(), kind=jnp.bfloat16):
    array = width * jax.random.normal(key, dims, jnp.float32)
    if pieces:
        array = array * steps_of(key, dims, pieces, -0.22, 0.18)
    return jnp.clip(array, -limit, limit).astype(kind)


def setup_inputs(seed: int = 0, part: int = 0) -> dict:
    seeds = jax.random.split(jax.random.key(seed), 4)
    part_splits = jax.random.split(jax.random.fold_in(seeds[3], part), 4)
    queries = normal_values(seeds[0], (NQ, LAYERS, D), 1.0, 6.0, ((0, 16),))
    inv_hessian = draw_inv_hessian(jax.random.fold_in(seeds[3], 71), part)
    train_grads = normal_values(part_splits[2], (TRAIN, LAYERS, D), (LAYERS * D) ** -0.5, 0.0625, ((0, 16),))
    return dict(queries=queries, inv_hessian=inv_hessian, train_grads=train_grads)


def reference(queries, inv_hessian, train_grads):
    layer_products = []
    for layer in range(LAYERS):
        layer_products.append(jnp.dot(queries[:, layer, :], inv_hessian[layer], preferred_element_type=jnp.float32))
    precond = jnp.stack(layer_products, axis=1).astype(jnp.bfloat16)
    flat_precond = precond.reshape(NQ, LAYERS * D)
    train_blocks = train_grads.reshape(N_DP, T_DEV, LAYERS * D)

    def score_block(train_rows):
        return jnp.dot(flat_precond, train_rows.T, preferred_element_type=jnp.float32)

    block_scores = lax.map(score_block, train_blocks)
    return jnp.transpose(block_scores, (1, 0, 2)).reshape(NQ, N_DP * T_DEV)
```

```python
import functools

import jax
import jax.numpy as jnp
from jax import lax
from jax.experimental import pallas as pl
from jax.experimental.pallas import tpu as pltpu
from jax.sharding import PartitionSpec as P

NT = (((1,), (1,)), ((), ()))


def dot_nt(a, b):
    return lax.dot_general(a, b, NT, preferred_element_type=jnp.float32)


def gather(n, buf, send_sem, recv_sem, me):
    line = n // 4
    z, y, c = me // 4, lax.rem(me // 2, 2), lax.rem(me, 2)

    def index(zz, yy, cc):
        return (zz * 2 + yy) * 2 + cc

    sends = []

    def send(slot, to):
        copy = pltpu.make_async_remote_copy(
            src_ref=buf.at[slot], dst_ref=buf.at[slot],
            send_sem=send_sem.at[len(sends)], recv_sem=recv_sem.at[slot],
            device_id={"dp": to}, device_id_type=pl.DeviceIdType.MESH)
        copy.start()
        sends.append(copy)

    def arrived(slot):
        pltpu.make_async_remote_copy(
            src_ref=buf.at[slot], dst_ref=buf.at[slot],
            send_sem=send_sem.at[0], recv_sem=recv_sem.at[slot],
            device_id={"dp": index(z, y, 1 - c)}, device_id_type=pl.DeviceIdType.MESH).wait_recv()

    zs = [lax.rem(z + d, line) for d in range(line)]
    across, other = index(z, 1 - y, c), index(z, y, 1 - c)
    for d in range(1, line):
        send(me, index(zs[d], y, c))
    send(me, across)
    send(me, other)
    for d in range(1, line):
        slot = index(zs[d], y, c)
        arrived(slot)
        send(slot, across)
        send(slot, other)
    for d in range(line):
        slot = index(zs[d], 1 - y, c)
        arrived(slot)
        send(slot, other)
    yield None
    for d in range(line):
        arrived(index(zs[d], y, 1 - c))
        arrived(index(zs[d], 1 - y, 1 - c))
    yield None
    for copy in sends:
        copy.wait_send()
    yield None


def kernel(n, q_hbm, h_hbm, x_hbm, o_ref, qv, qg, pg, hv, xv, acc, local_sem, qs, qr, ps, pr):
    me = lax.axis_index("dp")
    line = n // 4
    z, y, c = me // 4, lax.rem(me // 2, 2), lax.rem(me, 2)
    nq_local, layers, feats = qv.shape
    nq = nq_local * n
    rows = hv.shape[1]
    width = qg.shape[2]
    parts = feats // width

    load_q = pltpu.make_async_copy(q_hbm, qv, local_sem.at[0])
    load_h = pltpu.make_async_copy(h_hbm, hv, local_sem.at[1])
    load_x = pltpu.make_async_copy(x_hbm.reshape(xv.shape), xv, local_sem.at[2])
    load_q.start()
    load_h.start()
    load_x.start()

    barrier = pltpu.get_barrier_semaphore()
    peers = [(lax.rem(z + d, line) * 2 + y) * 2 + c for d in range(1, line)]
    peers += [(z * 2 + 1 - y) * 2 + c, (z * 2 + y) * 2 + 1 - c]
    for peer in peers:
        pl.semaphore_signal(barrier, inc=1, device_id={"dp": peer}, device_id_type=pl.DeviceIdType.MESH)

    load_q.wait()
    tiles = []
    for i in range(nq_local):
        v = qv[i].astype(jnp.float32)
        tiles.append(jnp.concatenate([v[:, k * width:(k + 1) * width] for k in range(parts)], axis=0))
    qg[me] = jnp.concatenate(tiles, axis=0).astype(jnp.bfloat16)
    pl.semaphore_wait(barrier, len(peers))

    steps = gather(n, qg, qs, qr, me)
    next(steps)
    total = nq * layers * parts
    ri = lax.broadcasted_iota(jnp.int32, (total, total), 0)
    ci = lax.broadcasted_iota(jnp.int32, (total, total), 1)
    pick = (lax.rem(ri, nq) * (layers * parts) + ri // nq == ci).astype(jnp.float32).astype(jnp.bfloat16)
    next(steps)
    load_h.wait()
    ordered = jnp.dot(pick, qg[...].reshape(total, width), preferred_element_type=jnp.float32).astype(jnp.bfloat16)
    for l in range(layers):
        block = jnp.zeros((nq, rows), jnp.float32)
        for k in range(parts):
            first = (k * layers + l) * nq
            block += dot_nt(ordered[first:first + nq], hv[l, :, k * width:(k + 1) * width])
        pg[me, l * nq:(l + 1) * nq, :] = block.astype(jnp.bfloat16)
    next(steps)

    def score(slot):
        cols = pl.ds(pl.multiple_of(slot * rows, rows), rows)
        acc[...] += dot_nt(xv[:, cols], pg[slot])

    steps = gather(n, pg, ps, pr, me)
    next(steps)
    load_x.wait()
    acc[...] = jnp.zeros_like(acc)

    @pl.loop(0, n // 2)
    def _(i):
        score(i * 2 + c)

    next(steps)

    @pl.loop(0, n // 2)
    def _(i):
        score(i * 2 + 1 - c)

    next(steps)
    t = o_ref.shape[1]
    result = acc[pl.ds(0, t, layers), :][:, 0:nq]
    for l in range(1, layers):
        result += acc[pl.ds(l, t, layers), :][:, l * nq:(l + 1) * nq]
    o_ref[...] = result.T


def fused(n, queries, inv_hessian, train_grads):
    nq_local, layers, feats = queries.shape
    rows = inv_hessian.shape[1]
    t = train_grads.shape[0]
    nq = nq_local * n
    held = 16
    width = nq_local * layers * feats // held
    return pl.pallas_call(
        functools.partial(kernel, n),
        out_shape=jax.ShapeDtypeStruct((nq, t), jnp.float32),
        in_specs=[pl.BlockSpec(memory_space=pl.ANY)] * 3,
        out_specs=pl.BlockSpec(memory_space=pltpu.VMEM),
        scratch_shapes=[
            pltpu.VMEM((nq_local, layers, feats), jnp.bfloat16),
            pltpu.VMEM((n, held, width), jnp.bfloat16),
            pltpu.VMEM((n, layers * nq, rows), jnp.bfloat16),
            pltpu.VMEM((layers, rows, feats), jnp.bfloat16),
            pltpu.VMEM((t * layers, feats), jnp.bfloat16),
            pltpu.VMEM((t * layers, layers * nq), jnp.float32),
            pltpu.SemaphoreType.DMA((3,)),
            pltpu.SemaphoreType.DMA((n,)),
            pltpu.SemaphoreType.DMA((n,)),
            pltpu.SemaphoreType.DMA((n,)),
            pltpu.SemaphoreType.DMA((n,)),
        ],
        compiler_params=pltpu.CompilerParams(
            collective_id=0, has_side_effects=True, vmem_limit_bytes=48 * 2**20),
        cost_estimate=pl.CostEstimate(
            flops=2 * nq * layers * feats * (rows + t),
            bytes_accessed=2 * layers * feats * (rows + t), transcendentals=0),
    )(queries, inv_hessian, train_grads)


def plain(queries, inv_hessian, train_grads):
    nq_local, layers, feats = queries.shape
    t = train_grads.shape[0]
    whole = lax.all_gather(queries, "dp", axis=0, tiled=True)
    piece = jnp.einsum("qlj,lrj->qlr", whole, inv_hessian, preferred_element_type=jnp.float32).astype(jnp.bfloat16)
    precond = lax.all_gather(piece, "dp", axis=2, tiled=True)
    return jnp.dot(precond.reshape(-1, layers * feats), train_grads.reshape(t, layers * feats).T,
                   preferred_element_type=jnp.float32)


def solution(mesh):
    n = mesh.shape["dp"]

    def per_device(queries, inv_hessian, train_grads):
        nq_local, layers, feats = queries.shape
        if n == 16 and nq_local == 2 and layers == 2 and feats == 16 * inv_hessian.shape[1]:
            return fused(n, queries, inv_hessian, train_grads)
        return plain(queries, inv_hessian, train_grads)

    return jax.shard_map(
        per_device,
        mesh=mesh,
        in_specs=(P("dp", None, None), P(None, "dp", None), P(("groups", "dp"), None, None)),
        out_specs=P(None, ("groups", "dp")),
        check_vma=False,
    )
```

```python
import functools

import jax
import jax.numpy as jnp
from jax import lax
from jax.experimental import pallas as pl
from jax.experimental.pallas import tpu as pltpu
from jax.sharding import PartitionSpec as P

NT = (((1,), (1,)), ((), ()))


def dot_nt(a, b):
    return lax.dot_general(a, b, NT, preferred_element_type=jnp.float32)


def index(z, y, c):
    return (z * 2 + y) * 2 + c


def place(me):
    z, y, c = me // 4, lax.rem(me // 2, 2), lax.rem(me, 2)
    return [z, z + 1 - 2 * lax.rem(z, 2), lax.rem(z + 2, 4), 3 - z], y, c


class Copies:
    def __init__(self, send_sem, recv_sem):
        self.send_sem, self.recv_sem, self.started = send_sem, recv_sem, []

    def copy(self, ref, arrival, to, k):
        return pltpu.make_async_remote_copy(
            src_ref=ref, dst_ref=ref, send_sem=self.send_sem.at[k], recv_sem=self.recv_sem.at[arrival],
            device_id=to, device_id_type=pl.DeviceIdType.MESH)

    def send(self, ref, arrival, to):
        copy = self.copy(ref, arrival, to, len(self.started))
        copy.start()
        self.started.append(copy)

    def arrived(self, ref, arrival, to):
        self.copy(ref, arrival, to, 0).wait_recv()

    def finish(self):
        for copy in self.started:
            copy.wait_send()


def gather_queries(buf, send_sem, recv_sem, group, me):
    zs, y, c = place(me)
    copies = Copies(send_sem, recv_sem)
    other = {"groups": group, "dp": index(zs[0], y, 1 - c)}
    chips = [(zs[0], 1 - y), (zs[1], y), (zs[1], 1 - y), (zs[2], y), (zs[3], y), (zs[2], 1 - y), (zs[3], 1 - y)]
    for z, yy in reversed(chips):
        copies.send(buf.at[me], me, {"groups": group, "dp": index(z, yy, c)})
    copies.send(buf.at[me], me, other)
    for z, yy in chips:
        slot = index(z, yy, c)
        copies.arrived(buf.at[slot], slot, other)
        copies.send(buf.at[slot], slot, other)
    for z, yy in [(zs[0], y)] + chips:
        slot = index(z, yy, 1 - c)
        copies.arrived(buf.at[slot], slot, other)
    return copies


def gather_precond(n, nq, buf, send_sem, recv_sem, group, me, use):
    zs, y, c = place(me)
    copies = Copies(send_sem, recv_sem)
    other = {"groups": group, "dp": index(zs[0], y, 1 - c)}
    across = {"groups": group, "dp": index(zs[0], 1 - y, c)}

    def half(slot, layer):
        return buf.at[slot, pl.ds(pl.multiple_of(layer * nq, nq), nq)]

    for z in reversed(zs):
        copies.send(half(me, group), group * n + me, {"groups": 1 - group, "dp": index(z, y, c)})
        if z is not zs[0]:
            copies.send(half(me, group), group * n + me, {"groups": group, "dp": index(z, y, c)})

    own = [index(z, y, c) for z in zs]
    far = [index(z, 1 - y, c) for z in zs]
    own_x = [index(z, y, 1 - c) for z in zs]
    far_x = [index(z, 1 - y, 1 - c) for z in zs]

    def take(slot):
        copies.arrived(buf.at[slot], slot, other)

    for j, slot in enumerate(own):
        copies.arrived(half(slot, 1 - group), (1 - group) * n + slot, other)
        if j:
            copies.arrived(half(slot, group), group * n + slot, other)
        copies.send(buf.at[slot], slot, across)
        copies.send(buf.at[slot], slot, other)
        if j:
            use(own[j - 1])
    take(own_x[0])
    use(own[3], own_x[0])
    take(far[0])
    copies.send(buf.at[far[0]], far[0], other)
    take(own_x[1])
    take(own_x[2])
    use(own_x[1], own_x[2])
    take(far[1])
    copies.send(buf.at[far[1]], far[1], other)
    take(own_x[3])
    use(own_x[3], far[0])
    take(far[2])
    copies.send(buf.at[far[2]], far[2], other)
    take(far_x[0])
    use(far[1], far_x[0])
    take(far[3])
    copies.send(buf.at[far[3]], far[3], other)
    take(far_x[1])
    use(far[2], far_x[1])
    take(far_x[2])
    use(far[3], far_x[2])
    take(far_x[3])
    use(far_x[3])
    return copies


def kernel(n, q_hbm, h_hbm, x_hbm, o_ref, qv, qg, pg, hv, xv, acc, local_sem, qs, qr, ps, pr):
    group, me = lax.axis_index("groups"), lax.axis_index("dp")
    nq_local, layers, feats = qv.shape
    nq = nq_local * n
    rows = hv.shape[0]
    width = qg.shape[2]
    parts = feats // width

    load_q = pltpu.make_async_copy(q_hbm, qv, local_sem.at[0])
    load_h = pltpu.make_async_copy(h_hbm.at[group], hv, local_sem.at[1])
    load_x = pltpu.make_async_copy(x_hbm.reshape(xv.shape), xv, local_sem.at[2])
    load_q.start()
    load_h.start()
    load_x.start()

    barrier = pltpu.get_barrier_semaphore()
    zs, y, c = place(me)
    peers = [(group, index(z, yy, c)) for z in zs for yy in (y, 1 - y)][1:]
    peers += [(1 - group, index(z, y, c)) for z in zs] + [(group, index(zs[0], y, 1 - c))]
    for peer in reversed(peers):
        pl.semaphore_signal(barrier, inc=1, device_id={"groups": peer[0], "dp": peer[1]},
                            device_id_type=pl.DeviceIdType.MESH)

    load_q.wait()
    tiles = []
    for i in range(nq_local):
        v = qv[i].astype(jnp.float32)
        v = jnp.where(group == 0, v[0:1], v[1:2])
        tiles += [v[:, k * width:(k + 1) * width] for k in range(parts)]
    qg[me] = jnp.concatenate(tiles, axis=0).astype(jnp.bfloat16)

    total = nq * parts
    ri = lax.broadcasted_iota(jnp.int32, (total, total), 0)
    ci = lax.broadcasted_iota(jnp.int32, (total, total), 1)
    pick = (lax.rem(ri, nq) * parts + ri // nq == ci).astype(jnp.float32).astype(jnp.bfloat16)
    acc[...] = jnp.zeros_like(acc)
    pl.semaphore_wait(barrier, len(peers))

    queries = gather_queries(qg, qs, qr, group, me)
    load_h.wait()
    ordered = jnp.dot(pick, qg[...].reshape(total, width), preferred_element_type=jnp.float32).astype(jnp.bfloat16)
    block = jnp.zeros((nq, rows), jnp.float32)
    for k in range(parts):
        block += dot_nt(ordered[k * nq:(k + 1) * nq], hv[:, k * width:(k + 1) * width])
    pg[me, pl.ds(pl.multiple_of(group * nq, nq), nq), :] = block.astype(jnp.bfloat16)
    load_x.wait()

    def score(*slots):
        acc[...] += sum(dot_nt(xv[:, pl.ds(pl.multiple_of(s * rows, rows), rows)], pg[s]) for s in slots)

    precond = gather_precond(n, nq, pg, ps, pr, group, me, score)
    t = o_ref.shape[1]
    result = acc[pl.ds(0, t, layers), :][:, 0:nq]
    for l in range(1, layers):
        result += acc[pl.ds(l, t, layers), :][:, l * nq:(l + 1) * nq]
    o_ref[...] = result.T
    queries.finish()
    precond.finish()


def fused(n, queries, inv_hessian, train_grads):
    nq_local, layers, feats = queries.shape
    rows = inv_hessian.shape[1]
    t = train_grads.shape[0]
    nq = nq_local * n
    held = 16
    width = nq_local * feats // held
    return pl.pallas_call(
        functools.partial(kernel, n),
        out_shape=jax.ShapeDtypeStruct((nq, t), jnp.float32),
        in_specs=[pl.BlockSpec(memory_space=pltpu.HBM)] * 3,
        out_specs=pl.BlockSpec(memory_space=pltpu.VMEM),
        scratch_shapes=[
            pltpu.VMEM((nq_local, layers, feats), jnp.bfloat16),
            pltpu.VMEM((n, held, width), jnp.bfloat16),
            pltpu.VMEM((n, layers * nq, rows), jnp.bfloat16),
            pltpu.VMEM((rows, feats), jnp.bfloat16),
            pltpu.VMEM((t * layers, feats), jnp.bfloat16),
            pltpu.VMEM((t * layers, layers * nq), jnp.float32),
            pltpu.SemaphoreType.DMA((3,)),
            pltpu.SemaphoreType.DMA((n,)),
            pltpu.SemaphoreType.DMA((n,)),
            pltpu.SemaphoreType.DMA((2 * n,)),
            pltpu.SemaphoreType.DMA((2 * n,)),
        ],
        compiler_params=pltpu.CompilerParams(
            collective_id=0, has_side_effects=True, vmem_limit_bytes=60 * 2**20),
        cost_estimate=pl.CostEstimate(
            flops=2 * nq * feats * (rows + layers * t),
            bytes_accessed=2 * feats * (rows + layers * t), transcendentals=0),
    )(queries, inv_hessian, train_grads)


def plain(queries, inv_hessian, train_grads):
    nq_local, layers, feats = queries.shape
    t = train_grads.shape[0]
    whole = lax.all_gather(queries, "dp", axis=0, tiled=True)
    piece = jnp.einsum("qlj,lrj->qlr", whole, inv_hessian, preferred_element_type=jnp.float32).astype(jnp.bfloat16)
    precond = lax.all_gather(piece, "dp", axis=2, tiled=True)
    return jnp.dot(precond.reshape(-1, layers * feats), train_grads.reshape(t, layers * feats).T,
                   preferred_element_type=jnp.float32)


def solution(mesh):
    n = mesh.shape["dp"]

    def per_device(queries, inv_hessian, train_grads):
        nq_local, layers, feats = queries.shape
        if n == 16 and mesh.shape["groups"] == 2 and nq_local == 2 and layers == 2 and feats == 16 * inv_hessian.shape[1]:
            return fused(n, queries, inv_hessian, train_grads)
        return plain(queries, inv_hessian, train_grads)

    return jax.shard_map(
        per_device,
        mesh=mesh,
        in_specs=(P("dp", None, None), P(None, "dp", None), P(("groups", "dp"), None, None)),
        out_specs=P(None, ("groups", "dp")),
        check_vma=False,
    )
```

```python
import functools

import jax
import jax.numpy as jnp
from jax import lax
from jax.experimental import pallas as pl
from jax.experimental.pallas import tpu as pltpu
from jax.sharding import PartitionSpec as P

NT = (((1,), (1,)), ((), ()))


def dot_nt(a, b):
    return lax.dot_general(a, b, NT, preferred_element_type=jnp.float32)


def index(z, y, c):
    return (z * 2 + y) * 2 + c


def place(me):
    z, y, c = me // 4, lax.rem(me // 2, 2), lax.rem(me, 2)
    return [z, z + 1 - 2 * lax.rem(z, 2), lax.rem(z + 2, 4), 3 - z], y, c


class Copies:
    def __init__(self, send_sem, recv_sem):
        self.send_sem, self.recv_sem, self.started = send_sem, recv_sem, []

    def copy(self, ref, arrival, to, k):
        return pltpu.make_async_remote_copy(
            src_ref=ref, dst_ref=ref, send_sem=self.send_sem.at[k], recv_sem=self.recv_sem.at[arrival],
            device_id=to, device_id_type=pl.DeviceIdType.MESH)

    def send(self, ref, arrival, to):
        copy = self.copy(ref, arrival, to, len(self.started))
        copy.start()
        self.started.append(copy)

    def arrived(self, ref, arrival, to):
        self.copy(ref, arrival, to, 0).wait_recv()

    def finish(self):
        for copy in self.started:
            copy.wait_send()


def gather_queries(buf, send_sem, recv_sem, group, me):
    zs, y, c = place(me)
    copies = Copies(send_sem, recv_sem)
    other = {"groups": group, "dp": index(zs[0], y, 1 - c)}
    chips = [(zs[0], 1 - y), (zs[1], y), (zs[1], 1 - y), (zs[2], y), (zs[3], y), (zs[2], 1 - y), (zs[3], 1 - y)]
    for z, yy in reversed(chips):
        copies.send(buf.at[me], me, {"groups": group, "dp": index(z, yy, c)})
    copies.send(buf.at[me], me, other)
    for z, yy in chips:
        slot = index(z, yy, c)
        copies.arrived(buf.at[slot], slot, other)
        copies.send(buf.at[slot], slot, other)
    for z, yy in [(zs[0], y)] + chips:
        slot = index(z, yy, 1 - c)
        copies.arrived(buf.at[slot], slot, other)
    return copies


def gather_precond(n, nq, buf, send_sem, recv_sem, group, me, use):
    zs, y, c = place(me)
    copies = Copies(send_sem, recv_sem)
    other = {"groups": group, "dp": index(zs[0], y, 1 - c)}
    across = {"groups": group, "dp": index(zs[0], 1 - y, c)}

    def half(slot, layer):
        return buf.at[slot, pl.ds(pl.multiple_of(layer * nq, nq), nq)]

    for z in zs:
        copies.send(half(me, group), group * n + me, {"groups": 1 - group, "dp": index(z, y, c)})
    for z in reversed(zs[1:]):
        copies.send(half(me, group), group * n + me, {"groups": group, "dp": index(z, y, c)})

    own = [index(z, y, c) for z in zs]
    far = [index(z, 1 - y, c) for z in zs]
    own_x = [index(z, y, 1 - c) for z in zs]
    far_x = [index(z, 1 - y, 1 - c) for z in zs]

    def take(slot):
        copies.arrived(buf.at[slot], slot, other)

    for j, slot in enumerate(own):
        copies.arrived(half(slot, 1 - group), (1 - group) * n + slot, other)
        if j:
            copies.arrived(half(slot, group), group * n + slot, other)
        copies.send(buf.at[slot], slot, across)
        copies.send(buf.at[slot], slot, other)
        if j:
            use(own[j - 1])
    take(own_x[0])
    use(own[3], own_x[0])
    take(far[0])
    copies.send(buf.at[far[0]], far[0], other)
    take(own_x[1])
    take(own_x[2])
    use(own_x[1], own_x[2])
    take(far[1])
    copies.send(buf.at[far[1]], far[1], other)
    take(own_x[3])
    use(own_x[3], far[0])
    take(far[2])
    copies.send(buf.at[far[2]], far[2], other)
    take(far_x[0])
    use(far[1], far_x[0])
    take(far[3])
    copies.send(buf.at[far[3]], far[3], other)
    take(far_x[1])
    use(far[2], far_x[1])
    take(far_x[2])
    use(far[3], far_x[2])
    take(far_x[3])
    use(far_x[3])
    return copies


def kernel(n, qv, h_hbm, x_hbm, o_ref, qg, pg, hv, xv, acc, local_sem, qs, qr, ps, pr):
    group, me = lax.axis_index("groups"), lax.axis_index("dp")
    nq_local, layers, feats = qv.shape
    nq = nq_local * n
    rows = hv.shape[0]
    width = qg.shape[2]
    parts = feats // width

    load_h = pltpu.make_async_copy(h_hbm.at[group], hv, local_sem.at[0])
    load_x = pltpu.make_async_copy(x_hbm.reshape(xv.shape), xv, local_sem.at[1])
    load_h.start()
    load_x.start()

    barrier = pltpu.get_barrier_semaphore()
    zs, y, c = place(me)
    peers = [(group, index(z, yy, c)) for z in zs for yy in (y, 1 - y)][1:]
    peers += [(1 - group, index(z, y, c)) for z in zs] + [(group, index(zs[0], y, 1 - c))]
    for peer in reversed(peers):
        pl.semaphore_signal(barrier, inc=1, device_id={"groups": peer[0], "dp": peer[1]},
                            device_id_type=pl.DeviceIdType.MESH)

    tiles = []
    for i in range(nq_local):
        v = qv[i].astype(jnp.float32)
        v = jnp.where(group == 0, v[0:1], v[1:2])
        tiles += [v[:, k * width:(k + 1) * width] for k in range(parts)]
    qg[me] = jnp.concatenate(tiles, axis=0).astype(jnp.bfloat16)

    total = nq * parts
    ri = lax.broadcasted_iota(jnp.int32, (total, total), 0)
    ci = lax.broadcasted_iota(jnp.int32, (total, total), 1)
    pick = (lax.rem(ri, nq) * parts + ri // nq == ci).astype(jnp.float32).astype(jnp.bfloat16)
    acc[...] = jnp.zeros_like(acc)
    pl.semaphore_wait(barrier, len(peers))

    queries = gather_queries(qg, qs, qr, group, me)
    load_h.wait()
    ordered = jnp.dot(pick, qg[...].reshape(total, width), preferred_element_type=jnp.float32).astype(jnp.bfloat16)
    block = jnp.zeros((nq, rows), jnp.float32)
    for k in range(parts):
        block += dot_nt(ordered[k * nq:(k + 1) * nq], hv[:, k * width:(k + 1) * width])
    pg[me, pl.ds(pl.multiple_of(group * nq, nq), nq), :] = block.astype(jnp.bfloat16)
    load_x.wait()

    def score(*slots):
        acc[...] += sum(dot_nt(xv[:, pl.ds(pl.multiple_of(s * rows, rows), rows)], pg[s]) for s in slots)

    precond = gather_precond(n, nq, pg, ps, pr, group, me, score)
    t = o_ref.shape[1]
    result = acc[pl.ds(0, t, layers), :][:, 0:nq]
    for l in range(1, layers):
        result += acc[pl.ds(l, t, layers), :][:, l * nq:(l + 1) * nq]
    o_ref[...] = result.T
    queries.finish()
    precond.finish()


def fused(n, queries, inv_hessian, train_grads):
    nq_local, layers, feats = queries.shape
    rows = inv_hessian.shape[1]
    t = train_grads.shape[0]
    nq = nq_local * n
    held = 16
    width = nq_local * feats // held
    return pl.pallas_call(
        functools.partial(kernel, n),
        out_shape=jax.ShapeDtypeStruct((nq, t), jnp.float32),
        in_specs=[pl.BlockSpec(memory_space=pltpu.VMEM)] + [pl.BlockSpec(memory_space=pltpu.HBM)] * 2,
        out_specs=pl.BlockSpec(memory_space=pltpu.VMEM),
        scratch_shapes=[
            pltpu.VMEM((n, held, width), jnp.bfloat16),
            pltpu.VMEM((n, layers * nq, rows), jnp.bfloat16),
            pltpu.VMEM((rows, feats), jnp.bfloat16),
            pltpu.VMEM((t * layers, feats), jnp.bfloat16),
            pltpu.VMEM((t * layers, layers * nq), jnp.float32),
            pltpu.SemaphoreType.DMA((2,)),
            pltpu.SemaphoreType.DMA((n,)),
            pltpu.SemaphoreType.DMA((n,)),
            pltpu.SemaphoreType.DMA((2 * n,)),
            pltpu.SemaphoreType.DMA((2 * n,)),
        ],
        compiler_params=pltpu.CompilerParams(
            collective_id=0, has_side_effects=True, vmem_limit_bytes=53 * 2**20),
        cost_estimate=pl.CostEstimate(
            flops=2 * nq * feats * (rows + layers * t),
            bytes_accessed=2 * feats * (rows + layers * t), transcendentals=0),
    )(queries, inv_hessian, train_grads)


def plain(queries, inv_hessian, train_grads):
    nq_local, layers, feats = queries.shape
    t = train_grads.shape[0]
    whole = lax.all_gather(queries, "dp", axis=0, tiled=True)
    piece = jnp.einsum("qlj,lrj->qlr", whole, inv_hessian, preferred_element_type=jnp.float32).astype(jnp.bfloat16)
    precond = lax.all_gather(piece, "dp", axis=2, tiled=True)
    return jnp.dot(precond.reshape(-1, layers * feats), train_grads.reshape(t, layers * feats).T,
                   preferred_element_type=jnp.float32)


def solution(mesh):
    n = mesh.shape["dp"]

    def per_device(queries, inv_hessian, train_grads):
        nq_local, layers, feats = queries.shape
        if n == 16 and mesh.shape["groups"] == 2 and nq_local == 2 and layers == 2 and feats == 16 * inv_hessian.shape[1]:
            return fused(n, queries, inv_hessian, train_grads)
        return plain(queries, inv_hessian, train_grads)

    return jax.shard_map(
        per_device,
        mesh=mesh,
        in_specs=(P("dp", None, None), P(None, "dp", None), P(("groups", "dp"), None, None)),
        out_specs=P(None, ("groups", "dp")),
        check_vma=False,
    )
```
